32 devices in a mesh: section: 2 (over core), dp: 16 (over z, y, x).
Axes of the slice: x: 2, y: 2, z: 4, core: 2. Of those that a mesh axis runs over, the one named last changes fastest.
Arguments:
- inputs: bfloat16 [2, 16, 512, 768], P(None, 'dp'), may hold values from -6 to 6
- segments: int32 [2, 16, 512], P(None, 'dp'), may hold values from 0 to 3, never falling along the last dimension, each value on 1 to 256 neighbouring positions
- expert_ids: int32 [2, 2, 16, 512, 1], P('section', None, 'dp'), may hold values from 0 to 15; in each aligned block of 512 rows (0 to 511, 512 to 1023, ..., all dimensions but the last counted through in order) at most 48 rows name the same one
- w_query: bfloat16 [2, 768, 768], P('section', 'dp'), may hold values from -0.02734375 to 0.02734375
- w_key: bfloat16 [2, 768, 768], P('section', 'dp'), may hold values from -0.21875 to 0.21875
- w_value: bfloat16 [2, 768, 768], P('section', 'dp'), may hold values from -0.21875 to 0.21875
- w_out_proj: bfloat16 [2, 768, 768], P('section', 'dp'), may hold values from -2.5 to 2.5
- w_router: bfloat16 [2, 768, 16], P('section', 'dp'), may hold values from -0.15625 to 0.15625
- attn_gain: bfloat16 [2, 768], P('section', 'dp'), may hold values from 0.5 to 1.5
- ffn_gain: bfloat16 [2, 768], P('section', 'dp'), may hold values from 0.5 to 1.5
- rel_table: float32 [2, 32, 12], P('section'), may hold values from -4 to 4
- w_expert_in: bfloat16 [2, 768, 49152], P('section', None, 'dp'), may hold values from -0.21875 to 0.21875
- w_expert_out: bfloat16 [2, 49152, 768], P('section', 'dp'), may hold values from -2.5 to 2.5
- grad_out: bfloat16 [2, 16, 512, 768], P(None, 'dp'), may hold values from -6 to 6
Outputs:
- layer_out: bfloat16 [2, 2, 16, 512, 768], P('section', None, 'dp')
- grad_in: bfloat16 [2, 2, 16, 512, 768], P('section', None, 'dp')
- grad_query: float32 [2, 768, 768], P('section', 'dp')
- grad_key: float32 [2, 768, 768], P('section', 'dp')
- grad_value: float32 [2, 768, 768], P('section', 'dp')
- grad_out_proj: float32 [2, 768, 768], P('section', 'dp')
- grad_router: float32 [2, 768, 16], P('section', 'dp')
- grad_attn_gain: float32 [2, 768], P('section', 'dp')
- grad_ffn_gain: float32 [2, 768], P('section', 'dp')
- grad_table: float32 [2, 32, 12], P('section')
- grad_expert_in: float32 [2, 768, 49152], P('section', None, 'dp')
- grad_expert_out: float32 [2, 49152, 768], P('section', 'dp')
The draws below stay inside these ranges and needn't reach their ends.
Inputs may be any that keep to these rules, and one draw needn't show every extreme that they name: `expert_ids`: in each aligned block of 512 rows (one index of dp, one micro-batch, one layer), no expert is named more than 48 times. `segments`: ids never fall along a sequence; a document has 1 to 256 tokens.
All inputs are finite; a program needn't handle non-finite values.
Results may differ from the reference program's by a relative error of at most 0.022.
Values may be sent and summed in bfloat16 or wider, within the bound.
A program may use at most 448 MiB of HBM per device.

```python
import math
import jax
import jax.numpy as jnp
import numpy as np
from jax import lax

D = 768
HEADS = 12
HEAD = 64
FF = 3072
EXPERTS = 16
BUCKETS = 32
LENGTH = 512
MICRO = 2
SEQ_MB = 1
SEQS = 16
CAP = 48
N_SECTION = 2


def steps_of(own_key, shape, shards, smallest, top_value):
    def one(dim, shards_of):
        steps = jax.random.uniform(jax.random.fold_in(jax.random.fold_in(own_key, 6), dim), (shards_of,), jnp.float32, smallest / len(shards), top_value / len(shards))
        return jnp.repeat(jnp.exp(steps), shape[dim] // shards_of).reshape((-1,) + (1,) * (len(shape) - dim - 1))

    factor_of = one(*shards[0])
    for cut in shards[1:]:
        factor_of = factor_of * one(*cut)
    return factor_of


def length_profile(amount, total, limit, slope):
    loads = [(1 << 20) // math.isqrt(standing ** slope) + 1 for standing in range(2, amount + 1)]
    spare, counts = total - limit - (amount - 1), [1] * (amount - 1)
    while spare > 0:
        movable = [i for i in range(amount - 1) if counts[i] < limit]
        mass, remaining = sum([loads[i] for i in movable]), spare
        for i in movable:
            more = min(limit - counts[i], max(1, remaining * loads[i] // mass), spare)
            counts[i] = counts[i] + more
            spare = spare - more
    return np.array([limit] + counts)


def ragged(rng, count, total, reach, slope):
    if count == 2:
        one = jax.random.randint(rng, (), max(1, total - reach), min(reach, total - 1) + 1)
        return jnp.stack([one, total - one])
    sizes = jnp.asarray(length_profile(count, total, reach, slope), jnp.int32)
    couples = (count - 1) // 2
    donor, sink = sizes[1:1 + 2 * couples:2], sizes[2:2 + 2 * couples:2]
    room = jnp.minimum(donor - 1, reach - sink)
    moved = jax.random.randint(jax.random.fold_in(rng, 1), (couples,), 0, 1 << 20) % (room + 1)
    sizes = sizes.at[1:1 + 2 * couples:2].set(donor - moved).at[2:2 + 2 * couples:2].set(sink + moved)
    return sizes[jax.random.permutation(jax.random.fold_in(rng, 2), count)]


def deal_out(rng, own, number, rows, number_of, top, most, slope):
    order = jax.random.permutation(rng, number_of)
    heavy_load, usual = load_shares(number_of, rows * top, most, slope, True), load_shares(number_of, rows * top, most, slope, False)
    places = jnp.arange(number_of)

    def named(tallies, offset_by):
        used = int((tallies > 0).sum())
        fixed = max(1, used // 4)
        moved = fixed + (places - fixed + offset_by * (used - fixed)) % max(1, number_of - fixed)
        return jnp.zeros((number_of,), jnp.int32).at[order[jnp.where(places < fixed, places, moved)]].set(jnp.asarray(tallies, jnp.int32))

    tallies = jnp.where(number % 4 == 0, named(heavy_load, number // 4), named(usual, number - number // 4 - 1))
    mixed = jax.random.permutation(jax.random.fold_in(own, 3), number_of)
    donor, sink = mixed[0:number_of // 2 * 2:2], mixed[1:number_of // 2 * 2:2]
    margin = jnp.minimum(tallies[donor] - 1, most - tallies[sink]) // 2
    margin = jnp.where((donor == order[0]) | (sink == order[0]) | (tallies[sink] == 0), 0, jnp.maximum(margin, 0))
    moved = jax.random.randint(jax.random.fold_in(own, 4), (number_of // 2,), 0, 1 << 20) % (margin + 1)
    tallies = tallies.at[donor].add(-moved).at[sink].add(moved)
    members = jnp.searchsorted(jnp.cumsum(tallies), jnp.arange(rows * top), side="right").astype(jnp.int32)
    grid = members.reshape(top, rows).T
    grid = grid[jax.random.permutation(jax.random.fold_in(own, 1), rows)]
    offset_by = jax.random.randint(jax.random.fold_in(own, 2), (rows, 1), 0, top)
    return jnp.take_along_axis(grid, (jnp.arange(top)[None, :] + offset_by) % top, axis=1)


def load_shares(amount, total, limit, lean, full):
    portions = [(1 << 20) // math.isqrt(standing ** lean) + 1 for standing in range(1, amount + 1)]
    largest = limit if full else min(limit, max(-(-total // amount), total * portions[0] // sum(portions)))
    least = 1 if total - largest >= amount - 1 else 0
    holding, rest = [largest] + [least] * (amount - 1), total - largest - least * (amount - 1)
    while rest > 0:
        candidates = [i for i in range(1, amount) if holding[i] < largest] or [i for i in range(1, amount) if holding[i] < limit]
        mass, remaining = sum([portions[i] for i in candidates]), rest
        for i in candidates:
            addition = min(limit - holding[i], max(1, remaining * portions[i] // mass), rest)
            holding[i] = holding[i] + addition
            rest = rest - addition
    return np.array(holding)


def bell_draw(rng, shape, scale, bound, cuts=(), held_as=jnp.bfloat16):
    loudness = steps_of(rng, shape, cuts, -0.22, 0.18) if cuts else 1.0
    array = jax.random.normal(rng, shape, jnp.float32) * scale * loudness
    return jnp.minimum(jnp.maximum(array, -bound), bound).astype(held_as)


def setup_inputs(seed: int = 0) -> dict:
    keys = jax.random.split(jax.random.key(seed), 15)
    inputs = bell_draw(keys[0], (MICRO, SEQS, LENGTH, D), 1.0, 6.0, ((1, 16),))
    segments = jax.vmap(lambda own: jnp.searchsorted(jnp.cumsum(ragged(own, 4, LENGTH, LENGTH // 2, 1)), jnp.arange(LENGTH), side="right"))(jax.random.split(keys[1], MICRO * SEQS)).reshape((MICRO, SEQS, LENGTH)).astype(jnp.int32)
    expert_ids_keys = jax.random.split(jax.random.fold_in(keys[2], 1), N_SECTION * MICRO * SEQS * LENGTH // (SEQ_MB * LENGTH))
    expert_ids_turns = jax.random.permutation(jax.random.fold_in(keys[2], 3), N_SECTION * MICRO * SEQS * LENGTH // (SEQ_MB * LENGTH))
    expert_ids = jax.vmap(lambda own, number: deal_out(jax.random.fold_in(keys[2], 2), own, number, SEQ_MB * LENGTH, EXPERTS, 1, CAP, 1))(expert_ids_keys, expert_ids_turns).reshape((N_SECTION, MICRO, SEQS, LENGTH, 1))
    w_query = bell_draw(keys[3], (N_SECTION, D, D), (D * HEAD) ** -0.5, 0.02734375, ((0, 2), (1, 16)))
    w_key = bell_draw(keys[4], (N_SECTION, D, D), D ** -0.5, 0.21875, ((0, 2), (1, 16)))
    w_value = bell_draw(keys[5], (N_SECTION, D, D), D ** -0.5, 0.21875, ((0, 2), (1, 16)))
    w_out_proj = bell_draw(keys[6], (N_SECTION, D, D), (max(D * 4 // LENGTH, 1)) ** -0.5, 2.5, ((0, 2), (1, 16)))
    w_router = bell_draw(keys[7], (N_SECTION, D, EXPERTS), (2 * D) ** -0.5, 0.15625, ((0, 2), (1, 16)))
    attn_gain = jnp.clip(1.0 + 0.1 * jax.random.normal(keys[8], (N_SECTION, D), jnp.float32), 0.5, 1.5).astype(jnp.bfloat16)
    ffn_gain = jnp.clip(1.0 + 0.1 * jax.random.normal(keys[9], (N_SECTION, D), jnp.float32), 0.5, 1.5).astype(jnp.bfloat16)
    rel_table = bell_draw(keys[10], (N_SECTION, BUCKETS, HEADS), 1.0, 4.0, ((0, 2),), jnp.float32)
    w_expert_in = bell_draw(keys[11], (N_SECTION, D, EXPERTS * FF), D ** -0.5, 0.21875, ((0, 2), (2, 16)))
    w_expert_out = bell_draw(keys[12], (N_SECTION, EXPERTS * FF, D), (max(FF // 512, 1)) ** -0.5, 2.5, ((0, 2), (1, 16)))
    grad_out = bell_draw(keys[13], (MICRO, SEQS, LENGTH, D), 1.0, 6.0, ((1, 16),))
    return {"inputs": inputs, "segments": segments, "expert_ids": expert_ids, "w_query": w_query, "w_key": w_key, "w_value": w_value, "w_out_proj": w_out_proj, "w_router": w_router, "attn_gain": attn_gain, "ffn_gain": ffn_gain, "rel_table": rel_table, "w_expert_in": w_expert_in, "w_expert_out": w_expert_out, "grad_out": grad_out}


@jax.custom_vjp
def low(v):
    return lax.optimization_barrier(v.astype(jnp.bfloat16)).astype(jnp.float32)

@jax.custom_vjp
def low_back(v):
    return v

def low_keep(v):
    return (low(v), None)

def low_pass(kept, grad):
    return (grad,)

def back_keep(v):
    return (v, None)

def back_low(kept, grad):
    return (low(grad),)
low.defvjp(low_keep, low_pass)
low_back.defvjp(back_keep, back_low)
norm_eps = 1e-06
distance_marks = (1, 2, 3, 4, 5, 6, 7, 8, 12, 16, 23, 32, 46, 64, 91)
highest = lax.Precision.HIGHEST

def normed(hidden, gain):
    return hidden * lax.rsqrt(lax.optimization_barrier(jnp.mean(hidden * hidden, axis=-1, keepdims=True)) + norm_eps) * gain

def bucket_of(offset):
    distance = jnp.abs(offset)
    bucket = jnp.zeros(offset.shape, jnp.int32)
    for marker in distance_marks:
        bucket = bucket + (distance >= marker).astype(jnp.int32)
    return bucket + BUCKETS // 2 * (offset > 0).astype(jnp.int32)

def product(left, right):
    return jnp.dot(left, right, precision=highest)

def attend_one(query, key_rows, value_rows, segment, bias):
    scores = jnp.einsum('qhd,khd->hqk', query, key_rows, precision=highest) + bias
    scores = low_back(scores)
    same_doc = segment[:, None] == segment[None, :]
    scores = jnp.where(same_doc[None], scores, -1e+30)
    attn_prob = low(jax.nn.softmax(scores, axis=-1))
    return jnp.einsum('hqk,khd->qhd', attn_prob, value_rows, precision=highest)

def expert_block(ffn_rows, expert_of, w_in, w_out):
    model_width = ffn_rows.shape[1]
    chosen = (expert_of[:, None] == jnp.arange(EXPERTS, dtype=jnp.int32)[None, :]).astype(jnp.int32)
    running = jnp.cumsum(chosen, axis=0).astype(jnp.int32)
    order_in = lax.optimization_barrier(jnp.sum((running - 1) * chosen, axis=1)).astype(jnp.int32)
    slots = (expert_of * CAP + order_in).astype(jnp.int32)
    buffer = jnp.zeros((EXPERTS * CAP, model_width), jnp.float32).at[slots].set(ffn_rows)
    buffer = low_back(buffer)
    hidden = jnp.einsum('ecd,def->ecf', buffer.reshape(EXPERTS, CAP, model_width), w_in.reshape(model_width, EXPERTS, FF), precision=highest)
    hidden = low_back(hidden)
    active = low(jax.nn.gelu(hidden))
    expert_sum = low_back(low(jnp.einsum('ecf,efd->ecd', active, w_out.reshape(EXPERTS, FF, model_width), precision=highest)))
    return jnp.take(expert_sum.reshape(EXPERTS * CAP, model_width), slots, axis=0)

def layer(params, hidden, segments, expert_of):
    w_q, w_k, w_v, w_o, w_r, gain_attn, gain_ffn, table, w_in, w_out = params
    micro_count, seq_count, length, model_width = hidden.shape
    flat_rows = hidden.reshape(-1, model_width)
    attn_in = low(normed(flat_rows, gain_attn))
    query = low_back(low(product(attn_in, w_q)))
    key_proj = low_back(low(product(attn_in, w_k)))
    value_proj = low_back(low(product(attn_in, w_v)))
    shape_heads = (micro_count * seq_count, length, HEADS, HEAD)
    positions = jnp.arange(length, dtype=jnp.int32)
    buckets = bucket_of(positions[None, :] - positions[:, None])
    bias = jnp.transpose(jnp.take(table, buckets, axis=0), (2, 0, 1))
    attend = jax.checkpoint(lambda operands: attend_one(operands[0], operands[1], operands[2], operands[3], bias))
    context = lax.map(attend, (query.reshape(shape_heads), key_proj.reshape(shape_heads), value_proj.reshape(shape_heads), segments.reshape(-1, length)))
    context = low_back(low(context.reshape(-1, model_width)))
    after_attn = flat_rows + low_back(product(context, w_o))
    ffn_in = low(normed(after_attn, gain_ffn))
    router_prob = jax.nn.softmax(low_back(product(ffn_in, w_r)), axis=-1)
    experts_flat = expert_of.reshape(-1)
    chosen = (experts_flat[:, None] == jnp.arange(EXPERTS, dtype=jnp.int32)[None, :]).astype(jnp.float32)
    gating = lax.optimization_barrier(jnp.sum(router_prob * chosen, axis=-1))
    block_rows = SEQ_MB * length
    routed = jax.checkpoint(lambda operands: expert_block(operands[0], operands[1], w_in, w_out))
    expert_rows = lax.map(routed, (ffn_in.reshape(-1, block_rows, model_width), experts_flat.reshape(-1, block_rows)))
    layer_result = after_attn + gating[:, None] * expert_rows.reshape(-1, model_width)
    return layer_result.reshape(hidden.shape)

def reference(inputs, segments, expert_ids, w_query, w_key, w_value, w_out_proj, w_router, attn_gain, ffn_gain, rel_table, w_expert_in, w_expert_out, grad_out):
    weights = (w_query, w_key, w_value, w_out_proj, w_router, attn_gain, ffn_gain, rel_table, w_expert_in, w_expert_out)
    first_params = tuple((weight[0].astype(jnp.float32) for weight in weights))
    second_params = tuple((weight[1].astype(jnp.float32) for weight in weights))
    routing = expert_ids[..., 0]

    def full_model(first, second, start, middle_tap):
        middle = low_back(low(layer(first, start, segments, routing[0])) + middle_tap)
        final = layer(second, middle, segments, routing[1])
        return (middle, final)
    start = inputs.astype(jnp.float32)
    (middle, final), pull_back = jax.vjp(full_model, first_params, second_params, start, jnp.zeros_like(start))
    first_grads, second_grads, start_grad, middle_grad = pull_back((jnp.zeros_like(middle), grad_out.astype(jnp.float32)))
    layer_out = jnp.stack([middle, final]).astype(jnp.bfloat16)
    grad_in = jnp.stack([start_grad, middle_grad]).astype(jnp.bfloat16)
    stacked = [jnp.stack([first_grad, second_grad]) for first_grad, second_grad in zip(first_grads, second_grads)]
    return (layer_out, grad_in, stacked[0], stacked[1], stacked[2], stacked[3], stacked[4], stacked[5], stacked[6], stacked[7], stacked[8], stacked[9])
```

```python
import jax
import jax.numpy as jnp
from jax import lax
from jax.experimental import pallas as pl
from jax.experimental.pallas import tpu as pltpu
from jax.sharding import PartitionSpec as P

EXPERTS = 16
BUCKETS = 32
CAP = 48


norm_eps = 1e-06
distance_marks = (1, 2, 3, 4, 5, 6, 7, 8, 12, 16, 23, 32, 46, 64, 91)
masked_score = -1e30
highest = lax.Precision.HIGHEST
kernel_params = pltpu.CompilerParams(vmem_limit_bytes=40 * 1024 * 1024)
LANES = 128
SUBLANES = 8


def normed(hidden, gain):
    return hidden * lax.rsqrt(jnp.mean(hidden * hidden, axis=-1, keepdims=True) + norm_eps) * gain


def bucket_of(offset):
    distance = jnp.abs(offset)
    bucket = jnp.zeros(offset.shape, jnp.int32)
    for marker in distance_marks:
        bucket = bucket + (distance >= marker).astype(jnp.int32)
    return bucket + BUCKETS // 2 * (offset > 0).astype(jnp.int32)


def one_hot_buckets(offsets):
    return (bucket_of(offsets)[..., None] == jnp.arange(BUCKETS, dtype=jnp.int32)).astype(
        jnp.float32
    )


def bias_kernel(line_ref, bias_ref):
    length = bias_ref.shape[1]
    rows = jnp.broadcast_to(line_ref[0], (length, 2 * length))
    bias_ref[0] = pltpu.roll(rows, 0, 1, stride=1, stride_axis=0)[:, :length]


def bias_of(table, length):
    heads = table.shape[1]
    turn = jnp.arange(2 * length, dtype=jnp.int32)
    offsets = jnp.where(turn < length, turn, turn - 2 * length)
    line = jnp.dot(one_hot_buckets(offsets), table, precision=highest).T[:, None, :]
    return pl.pallas_call(
        bias_kernel,
        grid=(heads,),
        in_specs=[pl.BlockSpec((1, 1, 2 * length), lambda h: (h, 0, 0))],
        out_specs=pl.BlockSpec((1, length, length), lambda h: (h, 0, 0)),
        out_shape=jax.ShapeDtypeStruct((heads, length, length), jnp.float32),
        compiler_params=kernel_params,
    )(line)


def contract(left, right, left_dim, right_dim):
    return lax.dot_general(
        left, right, (((left_dim,), (right_dim,)), ((), ())), preferred_element_type=jnp.float32
    )


def head_probs(query, key_rows, bias, same_doc):
    scores = contract(query, key_rows, 1, 1) + bias
    scores = jnp.where(same_doc, scores, masked_score)
    weight = jnp.exp(scores - jnp.max(scores, axis=-1, keepdims=True))
    return weight * (1.0 / jnp.sum(weight, axis=-1, keepdims=True))


def forward_kernel(head_size, q_ref, k_ref, v_ref, col_ref, row_ref, bias_ref, context_ref):
    same_doc = col_ref[...] == row_ref[...]
    lane = lax.broadcasted_iota(jnp.int32, q_ref.shape, 1)
    query, key_rows, value_rows = q_ref[...], k_ref[...], v_ref[...]
    result = jnp.zeros(q_ref.shape, jnp.float32)
    for half in range(LANES // head_size):
        own = lane // head_size == half
        prob = head_probs(
            jnp.where(own, query, jnp.zeros_like(query)), key_rows, bias_ref[half], same_doc
        )
        part = contract(prob.astype(jnp.bfloat16), value_rows, 1, 0)
        result = jnp.where(own, part, result)
    context_ref[...] = result.astype(jnp.bfloat16)


def backward_kernel(
    head_size,
    q_ref,
    k_ref,
    v_ref,
    grad_ref,
    col_ref,
    row_ref,
    bias_ref,
    dq_ref,
    dk_ref,
    dv_ref,
    offset_ref,
):
    length = q_ref.shape[0]
    same_doc = col_ref[...] == row_ref[...]
    lane = lax.broadcasted_iota(jnp.int32, q_ref.shape, 1)
    query, key_rows, value_rows, grad = q_ref[...], k_ref[...], v_ref[...], grad_ref[...]
    zero = jnp.zeros(q_ref.shape, jnp.float32)
    dq, dk, dv = zero, zero, zero
    for half in range(LANES // head_size):
        own = lane // head_size == half
        prob = head_probs(
            jnp.where(own, query, jnp.zeros_like(query)), key_rows, bias_ref[half], same_doc
        )
        dv = jnp.where(own, contract(prob.astype(jnp.bfloat16), grad, 0, 0), dv)
        prob_grad = contract(jnp.where(own, grad, jnp.zeros_like(grad)), value_rows, 1, 1)
        score_grad = prob * (prob_grad - jnp.sum(prob_grad * prob, axis=-1, keepdims=True))
        score_low = score_grad.astype(jnp.bfloat16)
        dq = jnp.where(own, contract(score_low, key_rows, 1, 0), dq)
        dk = jnp.where(own, contract(score_low, query, 0, 0), dk)
        rounded = score_low.astype(jnp.float32)
        columns = [jnp.zeros((SUBLANES, LANES), jnp.float32) for _ in range(2 * length // LANES)]
        pad = jnp.zeros((SUBLANES, LANES), jnp.float32)
        tiles = length // LANES
        for block in range(tiles):
            total = jnp.zeros((SUBLANES, length + LANES), jnp.float32)
            for step in range(LANES // SUBLANES):
                start = block * LANES + step * SUBLANES
                wide = jnp.concatenate([rounded[start : start + SUBLANES], pad], axis=1)
                total = total + pltpu.roll(wide, LANES - step * SUBLANES, 1)
            for tile in range(tiles + 1):
                place = tiles - 1 - block + tile
                columns[place] = columns[place] + total[:, tile * LANES : (tile + 1) * LANES]
        offset_ref[half] = jnp.concatenate(columns, axis=1)
    dq_ref[...] = dq.astype(jnp.bfloat16)
    dk_ref[...] = dk.astype(jnp.bfloat16)
    dv_ref[...] = dv.astype(jnp.bfloat16)


def attend_specs(length, width, heads, arrays):
    pair = heads * LANES // width
    wide = pl.BlockSpec((length, LANES), lambda h: (0, h))
    return wide, [wide] * arrays + [
        pl.BlockSpec((length, 1), lambda h: (0, 0)),
        pl.BlockSpec((1, length), lambda h: (0, 0)),
        pl.BlockSpec((pair, length, length), lambda h: (h, 0, 0)),
    ]


def attend_forward(query, key_rows, value_rows, segment, bias):
    length, width = query.shape
    heads = bias.shape[0]
    head_size = width // heads
    wide, in_specs = attend_specs(length, width, heads, 3)
    return pl.pallas_call(
        lambda *refs: forward_kernel(head_size, *refs),
        grid=(width // LANES,),
        in_specs=in_specs,
        out_specs=wide,
        out_shape=jax.ShapeDtypeStruct((length, width), jnp.bfloat16),
        compiler_params=kernel_params,
        cost_estimate=pl.CostEstimate(
            flops=4 * length * length * width,
            bytes_accessed=4 * heads * length * length,
            transcendentals=heads * length * length,
        ),
    )(query, key_rows, value_rows, segment[:, None], segment[None, :], bias)


def attend_backward(query, key_rows, value_rows, grad, segment, bias):
    length, width = query.shape
    heads = bias.shape[0]
    head_size = width // heads
    wide, in_specs = attend_specs(length, width, heads, 4)
    low = jax.ShapeDtypeStruct((length, width), jnp.bfloat16)
    return pl.pallas_call(
        lambda *refs: backward_kernel(head_size, *refs),
        grid=(width // LANES,),
        in_specs=in_specs,
        out_specs=[
            wide,
            wide,
            wide,
            pl.BlockSpec((LANES // head_size, SUBLANES, 2 * length), lambda h: (h, 0, 0)),
        ],
        out_shape=[
            low,
            low,
            low,
            jax.ShapeDtypeStruct((heads, SUBLANES, 2 * length), jnp.float32),
        ],
        compiler_params=kernel_params,
        cost_estimate=pl.CostEstimate(
            flops=10 * length * length * width,
            bytes_accessed=4 * heads * length * length,
            transcendentals=heads * length * length,
        ),
    )(query, key_rows, value_rows, grad, segment[:, None], segment[None, :], bias)


def table_sums(offset_sum):
    heads, rows, places = offset_sum.shape
    offsets = (
        jnp.arange(places, dtype=jnp.int32)[None, :]
        - places // 2
        - jnp.arange(rows, dtype=jnp.int32)[:, None]
    )
    chosen = one_hot_buckets(offsets).reshape(rows * places, BUCKETS)
    return jnp.dot(offset_sum.reshape(heads, rows * places), chosen, precision=highest).T


def dot32(left, right):
    return jnp.dot(left, right, preferred_element_type=jnp.float32)


def routes(expert_of):
    tokens = expert_of.shape[0]
    chosen = expert_of[:, None] == jnp.arange(EXPERTS, dtype=jnp.int32)[None, :]
    place = jnp.arange(tokens, dtype=jnp.int32)
    earlier = (place[:, None] > place[None, :]).astype(jnp.bfloat16)
    before = dot32(earlier, chosen.astype(jnp.bfloat16))
    order_in = jnp.sum(jnp.where(chosen, before, 0.0), axis=1).astype(jnp.int32)
    slots = expert_of * CAP + order_in
    spread = slots[:, None] == jnp.arange(EXPERTS * CAP, dtype=jnp.int32)[None, :]
    return chosen.astype(jnp.float32), spread.astype(jnp.bfloat16)


def swapped(value):
    return lax.ppermute(value, "section", [(0, 1), (1, 0)])


def local(
    inputs,
    segments,
    expert_ids,
    w_query,
    w_key,
    w_value,
    w_out_proj,
    w_router,
    attn_gain,
    ffn_gain,
    rel_table,
    w_expert_in,
    w_expert_out,
    grad_out,
):
    section = lax.axis_index("section")
    first = section == 0
    dp_size = lax.axis_size("dp")
    groups = dp_size // EXPERTS
    length, width = inputs.shape[2:]
    heads = rel_table.shape[2]
    shard_rows = w_query.shape[1]

    def by_micro(stacked):
        return lax.dynamic_index_in_dim(stacked, section, 0, keepdims=False)

    def of_layers(own, other):
        return jnp.where(first, own, other), jnp.where(first, other, own)

    small = jnp.concatenate(
        [
            w_router[0],
            attn_gain[0][:, None],
            ffn_gain[0][:, None],
            jnp.zeros((shard_rows, LANES - EXPERTS - 2), jnp.bfloat16),
        ],
        axis=1,
    )
    lead = jnp.concatenate([w_query[0], w_key[0], small], axis=1)
    rest = jnp.concatenate([w_value[0], w_out_proj[0], small], axis=1)
    shard_keep = jnp.where(first, lead, rest)
    shard_got = swapped(jnp.where(first, rest, lead))
    dense = []
    for shard in of_layers(shard_keep, shard_got):
        mine = lax.all_gather(shard, "dp", axis=0, tiled=True)
        theirs = swapped(mine)
        head_part, tail_part = of_layers(mine, theirs)
        dense.append(
            (
                head_part[:, :width],
                head_part[:, width : 2 * width],
                tail_part[:, :width],
                tail_part[:, width : 2 * width],
                head_part[:, 2 * width : 2 * width + EXPERTS],
                head_part[:, 2 * width + EXPERTS].astype(jnp.float32),
                head_part[:, 2 * width + EXPERTS + 1].astype(jnp.float32),
            )
        )

    segment = by_micro(segments)[0]
    ids = expert_ids[0, :, 0, :, 0]
    ids_keep = by_micro(ids)
    ids_got = swapped(lax.dynamic_index_in_dim(ids, 1 - section, 0, keepdims=False))
    routing = [routes(expert_of) for expert_of in of_layers(ids_keep, ids_got)]
    biases = [
        bias_of(table, length) for table in of_layers(rel_table[0], swapped(rel_table[0]))
    ]
    experts_in = of_layers(w_expert_in[0], swapped(w_expert_in[0]))
    experts_out = of_layers(w_expert_out[0], swapped(w_expert_out[0]))

    def exchanged(buffer):
        return lax.all_to_all(buffer, "dp", split_axis=0, concat_axis=0, tiled=True)

    def to_owners(rows):
        spread_rows = jnp.broadcast_to(
            rows.reshape(EXPERTS, 1, CAP, width), (EXPERTS, groups, CAP, width)
        )
        return exchanged(spread_rows.reshape(EXPERTS * groups, CAP, width)).reshape(-1, width)

    def from_owners(produced):
        returned = exchanged(
            produced.astype(jnp.bfloat16).reshape(EXPERTS * groups, CAP, width)
        ).astype(jnp.float32)
        return (
            jnp.sum(returned.reshape(EXPERTS, groups, CAP, width), axis=1)
            .reshape(EXPERTS * CAP, width)
            .astype(jnp.bfloat16)
        )

    def to_slots(spread, rows):
        return contract(spread, rows, 0, 0).astype(jnp.bfloat16)

    hidden_rows = by_micro(inputs)[0]
    layer_outs = []
    kept = []
    for layer in range(2):
        wq, wk, wv, wo, wr, gain_attn, gain_ffn = dense[layer]
        chosen, spread = routing[layer]
        layer_in = hidden_rows.astype(jnp.float32)
        attn_in = normed(layer_in, gain_attn).astype(jnp.bfloat16)
        query = dot32(attn_in, wq).astype(jnp.bfloat16)
        key_rows = dot32(attn_in, wk).astype(jnp.bfloat16)
        value_rows = dot32(attn_in, wv).astype(jnp.bfloat16)
        context = attend_forward(query, key_rows, value_rows, segment, biases[layer])
        after_attn = layer_in + dot32(context, wo)
        ffn_in = normed(after_attn, gain_ffn).astype(jnp.bfloat16)
        arrived = to_owners(to_slots(spread, ffn_in))
        router_prob = jax.nn.softmax(dot32(ffn_in, wr), axis=-1)
        gating = jnp.sum(router_prob * chosen, axis=-1)
        hidden = dot32(arrived, experts_in[layer])
        active = jax.nn.gelu(hidden).astype(jnp.bfloat16)
        expert_sum = from_owners(dot32(active, experts_out[layer]))
        expert_rows = dot32(spread, expert_sum)
        hidden_rows = (after_attn + gating[:, None] * expert_rows).astype(jnp.bfloat16)
        layer_outs.append(hidden_rows)
        kept.append(
            (
                layer_in,
                attn_in,
                query,
                key_rows,
                value_rows,
                context,
                after_attn,
                ffn_in,
                router_prob,
                gating,
                expert_rows,
                arrived,
                hidden,
                active,
            )
        )

    cotangent = by_micro(grad_out)[0]
    input_grads = [None, None]
    expert_grads = [None, None]
    dense_grads = [None, None]
    for layer in (1, 0):
        wq, wk, wv, wo, wr, gain_attn, gain_ffn = dense[layer]
        chosen, spread = routing[layer]
        (
            layer_in,
            attn_in,
            query,
            key_rows,
            value_rows,
            context,
            after_attn,
            ffn_in,
            router_prob,
            gating,
            expert_rows,
            arrived,
            hidden,
            active,
        ) = kept[layer]
        result_grad = cotangent.astype(jnp.float32)
        expert_grad = (result_grad * gating[:, None]).astype(jnp.bfloat16)
        arrived_grad = to_owners(to_slots(spread, expert_grad))
        gate_grad = jnp.sum(result_grad * expert_rows, axis=-1)
        logit_grad = (router_prob * (chosen - gating[:, None]) * gate_grad[:, None]).astype(
            jnp.bfloat16
        )
        active_grad = contract(arrived_grad, experts_out[layer], 1, 1)
        gelu_pull = jax.vjp(jax.nn.gelu, hidden)[1]
        hidden_grad = gelu_pull(active_grad)[0].astype(jnp.bfloat16)
        slot_grad = from_owners(contract(hidden_grad, experts_in[layer], 1, 1))
        grad_expert_out = contract(active, arrived_grad, 0, 0).astype(jnp.bfloat16)
        grad_expert_in = contract(arrived, hidden_grad, 0, 0).astype(jnp.bfloat16)
        route = [(1 - layer, layer)]
        expert_grads[layer] = (
            (grad_expert_in, lax.ppermute(grad_expert_in, "section", route)),
            (grad_expert_out, lax.ppermute(grad_expert_out, "section", route)),
        )
        ffn_in_grad = dot32(spread, slot_grad) + contract(logit_grad, wr, 1, 1)
        norm_pull = jax.vjp(normed, after_attn, gain_ffn)[1]
        residual_grad, sum_gain_ffn = norm_pull(ffn_in_grad)
        after_grad = result_grad + residual_grad
        attn_grad = after_grad.astype(jnp.bfloat16)
        context_grad = contract(attn_grad, wo, 1, 1).astype(jnp.bfloat16)
        query_grad, key_grad, value_grad, offset_sum = attend_backward(
            query, key_rows, value_rows, context_grad, segment, biases[layer]
        )
        attn_in_grad = (
            contract(query_grad, wq, 1, 1)
            + contract(key_grad, wk, 1, 1)
            + contract(value_grad, wv, 1, 1)
        )
        norm_pull = jax.vjp(normed, layer_in, gain_attn)[1]
        input_grad, sum_gain_attn = norm_pull(attn_in_grad)
        cotangent = (after_grad + input_grad).astype(jnp.bfloat16)
        input_grads[layer] = cotangent
        table_grad = table_sums(offset_sum)
        table_columns = -(-table_grad.size // shard_rows)
        table_block = jnp.pad(
            table_grad.reshape(-1), (0, table_columns * shard_rows - table_grad.size)
        ).reshape(shard_rows, table_columns)
        extra = jnp.concatenate(
            [
                contract(ffn_in, logit_grad, 0, 0),
                sum_gain_attn[:, None],
                sum_gain_ffn[:, None],
                jnp.tile(table_block, (dp_size, 1)),
            ],
            axis=1,
        )
        extra = jnp.pad(extra, ((0, 0), (0, -extra.shape[1] % LANES)))
        lead = jnp.concatenate(
            [contract(attn_in, query_grad, 0, 0), contract(attn_in, key_grad, 0, 0), extra], axis=1
        ).astype(jnp.bfloat16)
        rest = jnp.concatenate(
            [
                contract(attn_in, value_grad, 0, 0),
                contract(context, attn_grad, 0, 0),
                jnp.zeros_like(extra),
            ],
            axis=1,
        ).astype(jnp.bfloat16)
        got = swapped(jnp.where(first, rest, lead))
        both = jnp.where(first, lead, rest).astype(jnp.float32) + got.astype(jnp.float32)
        dense_grads[layer] = lax.psum_scatter(
            both.astype(jnp.bfloat16), "dp", scatter_dimension=0, tiled=True
        )

    def own_layer(pair):
        return jnp.where(first, pair[0], pair[1])

    def other_layer(pair):
        return jnp.where(first, pair[1], pair[0])

    def both_micros(pair):
        mine = own_layer(pair)
        theirs = swapped(other_layer(pair))
        return jnp.stack(of_layers(mine, theirs))[None, :, None]

    def expert_total(which):
        (part0, got0), (part1, got1) = expert_grads[0][which], expert_grads[1][which]
        total = own_layer((part0, part1)).astype(jnp.float32) + own_layer((got0, got1)).astype(
            jnp.float32
        )
        return total[None]

    mine = own_layer(dense_grads)
    theirs = swapped(other_layer(dense_grads))
    lead, rest = (part.astype(jnp.float32) for part in of_layers(mine, theirs))
    extra = lead[:, 2 * width :]
    table_count = BUCKETS * heads
    table_columns = -(-table_count // shard_rows)
    table = extra[:, EXPERTS + 2 : EXPERTS + 2 + table_columns].reshape(-1)[:table_count]
    return (
        both_micros(layer_outs),
        both_micros(input_grads),
        lead[None, :, :width],
        lead[None, :, width : 2 * width],
        rest[None, :, :width],
        rest[None, :, width : 2 * width],
        extra[None, :, :EXPERTS],
        extra[None, :, EXPERTS],
        extra[None, :, EXPERTS + 1],
        table.reshape(1, BUCKETS, heads),
        expert_total(0),
        expert_total(1),
    )


def solution(mesh):
    return jax.shard_map(
        local,
        mesh=mesh,
        in_specs=(
            P(None, "dp", None, None),
            P(None, "dp", None),
            P("section", None, "dp", None, None),
            P("section", "dp", None),
            P("section", "dp", None),
            P("section", "dp", None),
            P("section", "dp", None),
            P("section", "dp", None),
            P("section", "dp"),
            P("section", "dp"),
            P("section", None, None),
            P("section", None, "dp"),
            P("section", "dp", None),
            P(None, "dp", None, None),
        ),
        out_specs=(
            P("section", None, "dp", None, None),
            P("section", None, "dp", None, None),
            P("section", "dp", None),
            P("section", "dp", None),
            P("section", "dp", None),
            P("section", "dp", None),
            P("section", "dp", None),
            P("section", "dp"),
            P("section", "dp"),
            P("section", None, None),
            P("section", None, "dp"),
            P("section", "dp", None),
        ),
        check_vma=False,
    )
```

```python
import jax
import jax.numpy as jnp
from jax import lax
from jax.experimental import pallas as pl
from jax.experimental.pallas import tpu as pltpu
from jax.sharding import PartitionSpec as P

EXPERTS = 16
BUCKETS = 32
CAP = 48


norm_eps = 1e-06
distance_marks = (1, 2, 3, 4, 5, 6, 7, 8, 12, 16, 23, 32, 46, 64, 91)
masked_score = -1e30
highest = lax.Precision.HIGHEST
kernel_params = pltpu.CompilerParams(vmem_limit_bytes=40 * 1024 * 1024)
LANES = 128
SUBLANES = 8


def normed(hidden, gain):
    return hidden * lax.rsqrt(jnp.mean(hidden * hidden, axis=-1, keepdims=True) + norm_eps) * gain


def bucket_of(offset):
    distance = jnp.abs(offset)
    bucket = jnp.zeros(offset.shape, jnp.int32)
    for marker in distance_marks:
        bucket = bucket + (distance >= marker).astype(jnp.int32)
    return bucket + BUCKETS // 2 * (offset > 0).astype(jnp.int32)


def one_hot_buckets(offsets):
    return (bucket_of(offsets)[..., None] == jnp.arange(BUCKETS, dtype=jnp.int32)).astype(
        jnp.float32
    )


def bias_kernel(line_ref, bias_ref):
    length = bias_ref.shape[1]
    rows = jnp.broadcast_to(line_ref[0], (length, 2 * length))
    bias_ref[0] = pltpu.roll(rows, 0, 1, stride=1, stride_axis=0)[:, :length]


def bias_of(table, length):
    heads = table.shape[1]
    turn = jnp.arange(2 * length, dtype=jnp.int32)
    offsets = jnp.where(turn < length, turn, turn - 2 * length)
    line = jnp.dot(one_hot_buckets(offsets), table, precision=highest).T[:, None, :]
    return pl.pallas_call(
        bias_kernel,
        grid=(heads,),
        in_specs=[pl.BlockSpec((1, 1, 2 * length), lambda h: (h, 0, 0))],
        out_specs=pl.BlockSpec((1, length, length), lambda h: (h, 0, 0)),
        out_shape=jax.ShapeDtypeStruct((heads, length, length), jnp.float32),
        compiler_params=kernel_params,
    )(line)


def contract(left, right, left_dim, right_dim):
    return lax.dot_general(
        left, right, (((left_dim,), (right_dim,)), ((), ())), preferred_element_type=jnp.float32
    )


def head_probs(query, key_rows, bias, same_doc):
    scores = contract(query, key_rows, 1, 1) + bias
    scores = jnp.where(same_doc, scores, masked_score)
    weight = jnp.exp(scores - jnp.max(scores, axis=-1, keepdims=True))
    return weight * (1.0 / jnp.sum(weight, axis=-1, keepdims=True))


def forward_kernel(head_size, q_ref, k_ref, v_ref, col_ref, row_ref, bias_ref, context_ref):
    same_doc = col_ref[...] == row_ref[...]
    lane = lax.broadcasted_iota(jnp.int32, q_ref.shape, 1)
    query, key_rows, value_rows = q_ref[...], k_ref[...], v_ref[...]
    result = jnp.zeros(q_ref.shape, jnp.float32)
    for half in range(LANES // head_size):
        own = lane // head_size == half
        prob = head_probs(
            jnp.where(own, query, jnp.zeros_like(query)), key_rows, bias_ref[half], same_doc
        )
        part = contract(prob.astype(jnp.bfloat16), value_rows, 1, 0)
        result = jnp.where(own, part, result)
    context_ref[...] = result.astype(jnp.bfloat16)


def backward_kernel(
    head_size,
    q_ref,
    k_ref,
    v_ref,
    grad_ref,
    col_ref,
    row_ref,
    bias_ref,
    dq_ref,
    dk_ref,
    dv_ref,
    offset_ref,
):
    length = q_ref.shape[0]
    same_doc = col_ref[...] == row_ref[...]
    lane = lax.broadcasted_iota(jnp.int32, q_ref.shape, 1)
    query, key_rows, value_rows, grad = q_ref[...], k_ref[...], v_ref[...], grad_ref[...]
    zero = jnp.zeros(q_ref.shape, jnp.float32)
    dq, dk, dv = zero, zero, zero
    for half in range(LANES // head_size):
        own = lane // head_size == half
        prob = head_probs(
            jnp.where(own, query, jnp.zeros_like(query)), key_rows, bias_ref[half], same_doc
        )
        dv = jnp.where(own, contract(prob.astype(jnp.bfloat16), grad, 0, 0), dv)
        prob_grad = contract(jnp.where(own, grad, jnp.zeros_like(grad)), value_rows, 1, 1)
        score_grad = prob * (prob_grad - jnp.sum(prob_grad * prob, axis=-1, keepdims=True))
        score_low = score_grad.astype(jnp.bfloat16)
        dq = jnp.where(own, contract(score_low, key_rows, 1, 0), dq)
        dk = jnp.where(own, contract(score_low, query, 0, 0), dk)
        rounded = score_low.astype(jnp.float32)
        columns = [jnp.zeros((SUBLANES, LANES), jnp.float32) for _ in range(2 * length // LANES)]
        pad = jnp.zeros((SUBLANES, LANES), jnp.float32)
        tiles = length // LANES
        for block in range(tiles):
            total = jnp.zeros((SUBLANES, length + LANES), jnp.float32)
            for step in range(LANES // SUBLANES):
                start = block * LANES + step * SUBLANES
                wide = jnp.concatenate([rounded[start : start + SUBLANES], pad], axis=1)
                total = total + pltpu.roll(wide, LANES - step * SUBLANES, 1)
            for tile in range(tiles + 1):
                place = tiles - 1 - block + tile
                columns[place] = columns[place] + total[:, tile * LANES : (tile + 1) * LANES]
        offset_ref[half] = jnp.concatenate(columns, axis=1)
    dq_ref[...] = dq.astype(jnp.bfloat16)
    dk_ref[...] = dk.astype(jnp.bfloat16)
    dv_ref[...] = dv.astype(jnp.bfloat16)


def attend_specs(length, width, heads, arrays):
    pair = heads * LANES // width
    wide = pl.BlockSpec((length, LANES), lambda h: (0, h))
    return wide, [wide] * arrays + [
        pl.BlockSpec((length, 1), lambda h: (0, 0)),
        pl.BlockSpec((1, length), lambda h: (0, 0)),
        pl.BlockSpec((pair, length, length), lambda h: (h, 0, 0)),
    ]


def attend_forward(query, key_rows, value_rows, segment, bias):
    length, width = query.shape
    heads = bias.shape[0]
    head_size = width // heads
    wide, in_specs = attend_specs(length, width, heads, 3)
    return pl.pallas_call(
        lambda *refs: forward_kernel(head_size, *refs),
        grid=(width // LANES,),
        in_specs=in_specs,
        out_specs=wide,
        out_shape=jax.ShapeDtypeStruct((length, width), jnp.bfloat16),
        compiler_params=kernel_params,
        cost_estimate=pl.CostEstimate(
            flops=4 * length * length * width,
            bytes_accessed=4 * heads * length * length,
            transcendentals=heads * length * length,
        ),
    )(query, key_rows, value_rows, segment[:, None], segment[None, :], bias)


def attend_backward(query, key_rows, value_rows, grad, segment, bias):
    length, width = query.shape
    heads = bias.shape[0]
    head_size = width // heads
    wide, in_specs = attend_specs(length, width, heads, 4)
    low = jax.ShapeDtypeStruct((length, width), jnp.bfloat16)
    return pl.pallas_call(
        lambda *refs: backward_kernel(head_size, *refs),
        grid=(width // LANES,),
        in_specs=in_specs,
        out_specs=[
            wide,
            wide,
            wide,
            pl.BlockSpec((LANES // head_size, SUBLANES, 2 * length), lambda h: (h, 0, 0)),
        ],
        out_shape=[
            low,
            low,
            low,
            jax.ShapeDtypeStruct((heads, SUBLANES, 2 * length), jnp.float32),
        ],
        compiler_params=kernel_params,
        cost_estimate=pl.CostEstimate(
            flops=10 * length * length * width,
            bytes_accessed=4 * heads * length * length,
            transcendentals=heads * length * length,
        ),
    )(query, key_rows, value_rows, grad, segment[:, None], segment[None, :], bias)


def table_sums(offset_sum):
    heads, rows, places = offset_sum.shape
    offsets = (
        jnp.arange(places, dtype=jnp.int32)[None, :]
        - places // 2
        - jnp.arange(rows, dtype=jnp.int32)[:, None]
    )
    chosen = one_hot_buckets(offsets).reshape(rows * places, BUCKETS)
    return jnp.dot(offset_sum.reshape(heads, rows * places), chosen, precision=highest).T


def dot32(left, right):
    return jnp.dot(left, right, preferred_element_type=jnp.float32)


def routes(expert_of):
    tokens = expert_of.shape[0]
    chosen = expert_of[:, None] == jnp.arange(EXPERTS, dtype=jnp.int32)[None, :]
    place = jnp.arange(tokens, dtype=jnp.int32)
    earlier = (place[:, None] > place[None, :]).astype(jnp.bfloat16)
    before = dot32(earlier, chosen.astype(jnp.bfloat16))
    order_in = jnp.sum(jnp.where(chosen, before, 0.0), axis=1).astype(jnp.int32)
    slots = expert_of * CAP + order_in
    spread = slots[:, None] == jnp.arange(EXPERTS * CAP, dtype=jnp.int32)[None, :]
    return chosen.astype(jnp.float32), spread.astype(jnp.bfloat16)


def swapped(value):
    return lax.ppermute(value, "section", [(0, 1), (1, 0)])


def local(
    inputs,
    segments,
    expert_ids,
    w_query,
    w_key,
    w_value,
    w_out_proj,
    w_router,
    attn_gain,
    ffn_gain,
    rel_table,
    w_expert_in,
    w_expert_out,
    grad_out,
):
    section = lax.axis_index("section")
    first = section == 0
    dp_size = lax.axis_size("dp")
    groups = dp_size // EXPERTS
    length, width = inputs.shape[2:]
    heads = rel_table.shape[2]
    shard_rows = w_query.shape[1]

    def by_micro(stacked):
        return lax.dynamic_index_in_dim(stacked, section, 0, keepdims=False)

    def of_layers(own, other):
        return jnp.where(first, own, other), jnp.where(first, other, own)

    small = jnp.concatenate(
        [
            w_router[0],
            attn_gain[0][:, None],
            ffn_gain[0][:, None],
            jnp.zeros((shard_rows, LANES - EXPERTS - 2), jnp.bfloat16),
        ],
        axis=1,
    )
    lead = jnp.concatenate([w_query[0], w_key[0], small], axis=1)
    rest = jnp.concatenate([w_value[0], w_out_proj[0], small], axis=1)
    shard_keep = jnp.where(first, lead, rest)
    shard_got = swapped(jnp.where(first, rest, lead))
    dense = []
    for shard in of_layers(shard_keep, shard_got):
        mine = lax.all_gather(shard, "dp", axis=0, tiled=True)
        theirs = swapped(mine)
        head_part, tail_part = of_layers(mine, theirs)
        dense.append(
            (
                head_part[:, :width],
                head_part[:, width : 2 * width],
                tail_part[:, :width],
                tail_part[:, width : 2 * width],
                head_part[:, 2 * width : 2 * width + EXPERTS],
                head_part[:, 2 * width + EXPERTS].astype(jnp.float32),
                head_part[:, 2 * width + EXPERTS + 1].astype(jnp.float32),
            )
        )

    segment = by_micro(segments)[0]
    ids = expert_ids[0, :, 0, :, 0]
    ids_keep = by_micro(ids)
    ids_got = swapped(lax.dynamic_index_in_dim(ids, 1 - section, 0, keepdims=False))
    routing = [routes(expert_of) for expert_of in of_layers(ids_keep, ids_got)]
    biases = [
        bias_of(table, length) for table in of_layers(rel_table[0], swapped(rel_table[0]))
    ]
    experts_in = of_layers(w_expert_in[0], swapped(w_expert_in[0]))
    experts_out = of_layers(w_expert_out[0], swapped(w_expert_out[0]))

    def exchanged(buffer):
        return lax.all_to_all(buffer, "dp", split_axis=0, concat_axis=0, tiled=True)

    def to_owners(rows):
        spread_rows = jnp.broadcast_to(
            rows.reshape(EXPERTS, 1, CAP, width), (EXPERTS, groups, CAP, width)
        )
        return exchanged(spread_rows.reshape(EXPERTS * groups, CAP, width)).reshape(-1, width)

    def from_owners(produced):
        returned = exchanged(
            produced.astype(jnp.bfloat16).reshape(EXPERTS * groups, CAP, width)
        ).astype(jnp.float32)
        return (
            jnp.sum(returned.reshape(EXPERTS, groups, CAP, width), axis=1)
            .reshape(EXPERTS * CAP, width)
            .astype(jnp.bfloat16)
        )

    def to_slots(spread, rows):
        return contract(spread, rows, 0, 0).astype(jnp.bfloat16)

    hidden_rows = by_micro(inputs)[0]
    layer_outs = []
    kept = []
    for layer in range(2):
        wq, wk, wv, wo, wr, gain_attn, gain_ffn = dense[layer]
        chosen, spread = routing[layer]
        layer_in = hidden_rows.astype(jnp.float32)
        attn_in = normed(layer_in, gain_attn).astype(jnp.bfloat16)
        query = dot32(attn_in, wq).astype(jnp.bfloat16)
        key_rows = dot32(attn_in, wk).astype(jnp.bfloat16)
        value_rows = dot32(attn_in, wv).astype(jnp.bfloat16)
        context = attend_forward(query, key_rows, value_rows, segment, biases[layer])
        after_attn = layer_in + dot32(context, wo)
        ffn_in = normed(after_attn, gain_ffn).astype(jnp.bfloat16)
        arrived = to_owners(to_slots(spread, ffn_in))
        router_prob = jax.nn.softmax(dot32(ffn_in, wr), axis=-1)
        gating = jnp.sum(router_prob * chosen, axis=-1)
        hidden = dot32(arrived, experts_in[layer])
        active = jax.nn.gelu(hidden).astype(jnp.bfloat16)
        expert_sum = from_owners(dot32(active, experts_out[layer]))
        expert_rows = dot32(spread, expert_sum)
        hidden_rows = (after_attn + gating[:, None] * expert_rows).astype(jnp.bfloat16)
        layer_outs.append(hidden_rows)
        kept.append(
            (
                layer_in,
                attn_in,
                query,
                key_rows,
                value_rows,
                context,
                after_attn,
                ffn_in,
                router_prob,
                gating,
                expert_rows,
                arrived,
                hidden,
                active,
            )
        )

    cotangent = by_micro(grad_out)[0]
    input_grads = [None, None]
    expert_grads = [None, None]
    dense_grads = [None, None]
    for layer in (1, 0):
        wq, wk, wv, wo, wr, gain_attn, gain_ffn = dense[layer]
        chosen, spread = routing[layer]
        (
            layer_in,
            attn_in,
            query,
            key_rows,
            value_rows,
            context,
            after_attn,
            ffn_in,
            router_prob,
            gating,
            expert_rows,
            arrived,
            hidden,
            active,
        ) = kept[layer]
        result_grad = cotangent.astype(jnp.float32)
        expert_grad = (result_grad * gating[:, None]).astype(jnp.bfloat16)
        arrived_grad = to_owners(to_slots(spread, expert_grad))
        gate_grad = jnp.sum(result_grad * expert_rows, axis=-1)
        logit_grad = (router_prob * (chosen - gating[:, None]) * gate_grad[:, None]).astype(
            jnp.bfloat16
        )
        active_grad = contract(arrived_grad, experts_out[layer], 1, 1)
        gelu_pull = jax.vjp(jax.nn.gelu, hidden)[1]
        hidden_grad = gelu_pull(active_grad)[0].astype(jnp.bfloat16)
        slot_grad = from_owners(contract(hidden_grad, experts_in[layer], 1, 1))
        grad_expert_out = contract(active, arrived_grad, 0, 0).astype(jnp.bfloat16)
        grad_expert_in = contract(arrived, hidden_grad, 0, 0).astype(jnp.bfloat16)
        route = [(1 - layer, layer)]
        expert_grads[layer] = (
            (grad_expert_in, lax.ppermute(grad_expert_in, "section", route)),
            (grad_expert_out, lax.ppermute(grad_expert_out, "section", route)),
        )
        ffn_in_grad = dot32(spread, slot_grad) + contract(logit_grad, wr, 1, 1)
        norm_pull = jax.vjp(normed, after_attn, gain_ffn)[1]
        residual_grad, sum_gain_ffn = norm_pull(ffn_in_grad)
        after_grad = result_grad + residual_grad
        attn_grad = after_grad.astype(jnp.bfloat16)
        context_grad = contract(attn_grad, wo, 1, 1).astype(jnp.bfloat16)
        query_grad, key_grad, value_grad, offset_sum = attend_backward(
            query, key_rows, value_rows, context_grad, segment, biases[layer]
        )
        attn_in_grad = (
            contract(query_grad, wq, 1, 1)
            + contract(key_grad, wk, 1, 1)
            + contract(value_grad, wv, 1, 1)
        )
        norm_pull = jax.vjp(normed, layer_in, gain_attn)[1]
        input_grad, sum_gain_attn = norm_pull(attn_in_grad)
        cotangent = (after_grad + input_grad).astype(jnp.bfloat16)
        input_grads[layer] = cotangent
        table_grad = table_sums(offset_sum)
        table_columns = -(-table_grad.size // shard_rows)
        table_block = jnp.pad(
            table_grad.reshape(-1), (0, table_columns * shard_rows - table_grad.size)
        ).reshape(shard_rows, table_columns)
        extra = jnp.concatenate(
            [
                contract(ffn_in, logit_grad, 0, 0),
                sum_gain_attn[:, None],
                sum_gain_ffn[:, None],
                jnp.tile(table_block, (dp_size, 1)),
            ],
            axis=1,
        )
        extra = jnp.pad(extra, ((0, 0), (0, -extra.shape[1] % LANES)))
        lead = jnp.concatenate(
            [contract(attn_in, query_grad, 0, 0), contract(attn_in, key_grad, 0, 0), extra], axis=1
        ).astype(jnp.bfloat16)
        rest = jnp.concatenate(
            [
                contract(attn_in, value_grad, 0, 0),
                contract(context, attn_grad, 0, 0),
                jnp.zeros_like(extra),
            ],
            axis=1,
        ).astype(jnp.bfloat16)
        got = swapped(jnp.where(first, rest, lead))
        both = jnp.where(first, lead, rest).astype(jnp.float32) + got.astype(jnp.float32)
        parts = exchanged(both.astype(jnp.bfloat16).reshape(dp_size, shard_rows, -1))
        dense_grads[layer] = jnp.sum(parts.astype(jnp.float32), axis=0)

    def own_layer(pair):
        return jnp.where(first, pair[0], pair[1])

    def other_layer(pair):
        return jnp.where(first, pair[1], pair[0])

    def both_micros(pair):
        mine = own_layer(pair)
        theirs = swapped(other_layer(pair))
        return jnp.stack(of_layers(mine, theirs))[None, :, None]

    def expert_total(which):
        (part0, got0), (part1, got1) = expert_grads[0][which], expert_grads[1][which]
        total = own_layer((part0, part1)).astype(jnp.float32) + own_layer((got0, got1)).astype(
            jnp.float32
        )
        return total[None]

    mine = own_layer(dense_grads)
    theirs = swapped(other_layer(dense_grads))
    lead, rest = (part.astype(jnp.float32) for part in of_layers(mine, theirs))
    extra = lead[:, 2 * width :]
    table_count = BUCKETS * heads
    table_columns = -(-table_count // shard_rows)
    table = extra[:, EXPERTS + 2 : EXPERTS + 2 + table_columns].reshape(-1)[:table_count]
    return (
        both_micros(layer_outs),
        both_micros(input_grads),
        lead[None, :, :width],
        lead[None, :, width : 2 * width],
        rest[None, :, :width],
        rest[None, :, width : 2 * width],
        extra[None, :, :EXPERTS],
        extra[None, :, EXPERTS],
        extra[None, :, EXPERTS + 1],
        table.reshape(1, BUCKETS, heads),
        expert_total(0),
        expert_total(1),
    )


def solution(mesh):
    return jax.shard_map(
        local,
        mesh=mesh,
        in_specs=(
            P(None, "dp", None, None),
            P(None, "dp", None),
            P("section", None, "dp", None, None),
            P("section", "dp", None),
            P("section", "dp", None),
            P("section", "dp", None),
            P("section", "dp", None),
            P("section", "dp", None),
            P("section", "dp"),
            P("section", "dp"),
            P("section", None, None),
            P("section", None, "dp"),
            P("section", "dp", None),
            P(None, "dp", None, None),
        ),
        out_specs=(
            P("section", None, "dp", None, None),
            P("section", None, "dp", None, None),
            P("section", "dp", None),
            P("section", "dp", None),
            P("section", "dp", None),
            P("section", "dp", None),
            P("section", "dp", None),
            P("section", "dp"),
            P("section", "dp"),
            P("section", None, None),
            P("section", None, "dp"),
            P("section", "dp", None),
        ),
        check_vma=False,
    )
```
